512 devices in a mesh: grp: 8 (over y_hi, core), seq: 64 (over z, x, y_lo).
Axes of the slice: x: 4, y: 8 (y_hi: 4, y_lo: 2; y = y_hi * 2 + y_lo), z: 8, core: 2. Of those that a mesh axis runs over, the one named last changes fastest.
Arguments:
- queries: bfloat16 [64, 24, 256, 128], P('grp', None, 'seq'), may hold values from -8 to 8
- keys: bfloat16 [64, 24, 256, 128], P('grp', None, 'seq'), may hold values from -6 to 6
- values: bfloat16 [64, 24, 256, 128], P('grp', None, 'seq'), may hold values from -6 to 6
- context: bfloat16 [256, 4096], P(None, 'grp'), may hold values from -6 to 6
- residual: bfloat16 [256, 4096], P('grp', 'seq'), may hold values from -6 to 6
- codes: int32 [4096, 4096], P('grp', 'seq'), may hold values from -127 to 127
- scales: float32 [32, 4096], P('grp', 'seq'), may hold values from 0.0001 to 0.0004
- gain: float32 [4096], P('seq'), may hold values from 0.5 to 1.5
- kv_weight: bfloat16 [4096, 6144], P(None, 'seq'), may hold values from -1 to 1
- lengths: int32 [4], replicated, may hold values from 1 to 64, 160 in all
Outputs:
- attended: bfloat16 [64, 24, 256, 128], P('grp', None, 'seq')
The draws below stay inside these ranges and needn't reach their ends.
Inputs may be any that keep to these rules, and one draw needn't show every extreme that they name: The lengths sum to 160 and one of them is exactly 64.
All inputs are finite; a program needn't handle non-finite values.
Results may differ from the reference program's by a relative error of at most 0.0071.
Values may be sent and summed in bfloat16 or wider, within the bound.
A program may use at most 64 MiB of HBM per device.

```python
import math
import jax
import jax.numpy as jnp
import numpy as np
from jax import lax

D_TEXT = 4096
QGROUP = 128
HEADS = 24
HEAD_DIM = 128
PROMPTS = 4
TLEN = 64
D = 3072
SAMPLES = 64
LENGTH = 256
TEXT_ROWS = 256


def draw_queries(key, part):
    key = jax.random.fold_in(key, 11)
    shape = (SAMPLES, HEADS, LENGTH, HEAD_DIM)
    base = jnp.clip(jax.random.normal(key, shape, jnp.float32), -6.0, 6.0)
    return base.astype(jnp.bfloat16)


def draw_keys(key, part):
    key = jax.random.fold_in(key, 12)
    shape = (SAMPLES, HEADS, LENGTH, HEAD_DIM)
    base = jnp.clip(jax.random.normal(key, shape, jnp.float32), -6.0, 6.0)
    return base.astype(jnp.bfloat16)


def draw_residual(key, part):
    key = jax.random.fold_in(key, 13)
    shape = (TEXT_ROWS, D_TEXT)
    base = jnp.clip(jax.random.normal(key, shape, jnp.float32), -6.0, 6.0)
    return base.astype(jnp.bfloat16)


def draw_kv_weight(key, part):
    key = jax.random.fold_in(key, 14)
    shape = (D_TEXT, 2 * D)
    factor = 1.0 / math.sqrt(D_TEXT)
    base = jnp.clip(jax.random.normal(key, shape, jnp.float32), -6.0, 6.0) * factor
    return base.astype(jnp.bfloat16)


def plant(drawn, rng, low, top_value):
    spot = [jax.random.randint(jax.random.fold_in(rng, axis), (), 0, length) for axis, length in enumerate(drawn.shape)]
    main_axis = drawn.shape.index(max(drawn.shape))
    beside = spot[:main_axis] + [(spot[main_axis] + 1) % drawn.shape[main_axis]] + spot[main_axis + 1:]
    return drawn.at[tuple(spot)].set(low).at[tuple(beside)].set(top_value)


def steps_of(own_key, shape, split, least, high):
    level = 1.0
    for axis_at, blocks in split:
        steps = jax.random.uniform(jax.random.fold_in(jax.random.fold_in(own_key, 6), axis_at), (blocks,), jnp.float32, least / len(split), high / len(split))
        level = level * jnp.repeat(jnp.exp(steps), shape[axis_at] // blocks).reshape((-1,) + (1,) * (len(shape) - 1 - axis_at))
    return level


def split_up(amount, total, most, lean):
    weights = [(1 << 20) // math.isqrt(rank ** lean) + 1 for rank in range(2, amount + 1)]
    rest, counts = total - most - (amount - 1), [1] * (amount - 1)
    while rest > 0:
        candidates = [i for i in range(amount - 1) if counts[i] < most]
        pool, remaining = sum([weights[i] for i in candidates]), rest
        for i in candidates:
            addition = min(most - counts[i], max(1, remaining * weights[i] // pool), rest)
            counts[i] = counts[i] + addition
            rest = rest - addition
    return np.array([most] + counts)


def ragged_sizes(own_key, number_of, total, limit, slope):
    if number_of == 2:
        one = jax.random.randint(own_key, (), max(1, total - limit), min(limit, total - 1) + 1)
        return jnp.stack([one, total - one])
    tallies = jnp.asarray(split_up(number_of, total, limit, slope), jnp.int32)
    pairs = (number_of - 1) // 2
    donor, taker = tallies[1:1 + 2 * pairs:2], tallies[2:2 + 2 * pairs:2]
    margin = jnp.minimum(donor - 1, limit - taker)
    passed = jax.random.randint(jax.random.fold_in(own_key, 1), (pairs,), 0, 1 << 20) % (margin + 1)
    tallies = tallies.at[1:1 + 2 * pairs:2].set(donor - passed).at[2:2 + 2 * pairs:2].set(taker + passed)
    return tallies[jax.random.permutation(jax.random.fold_in(own_key, 2), number_of)]


def bell_draw(own_key, dims, width, most, pieces=(), held_as=jnp.bfloat16):
    drawn = width * jax.random.normal(own_key, dims, jnp.float32)
    if pieces:
        drawn = drawn * steps_of(own_key, dims, pieces, -0.22, 0.18)
    return jnp.clip(drawn, -most, most).astype(held_as)


def setup_inputs(seed: int = 0) -> dict:
    seeds = jax.random.split(jax.random.key(seed), 11)
    queries = draw_queries(jax.random.fold_in(seeds[10], 71), 0)
    keys = draw_keys(jax.random.fold_in(seeds[10], 71), 0)
    values = bell_draw(seeds[2], (SAMPLES, HEADS, LENGTH, HEAD_DIM), 1.0, 6.0, ((0, 8), (2, 64)))
    context = bell_draw(seeds[3], (TEXT_ROWS, D_TEXT), 1.0, 6.0, ((1, 8),))
    residual = draw_residual(jax.random.fold_in(seeds[10], 71), 0)
    codes = plant(jax.random.randint(seeds[5], (D_TEXT, D_TEXT), -127, 128), jax.random.fold_in(seeds[5], 1), -127, 127).astype(jnp.int32)
    scales = jnp.clip(jnp.exp(math.log(0.0004) - 1.3862944 * jax.random.uniform(seeds[6], (D_TEXT // QGROUP, D_TEXT), jnp.float32) ** steps_of(seeds[6], (D_TEXT // QGROUP, D_TEXT), ((0, 8), (1, 64)), -0.2, 0.2)), 0.0001, 0.0004)
    gain = jnp.clip(1.0 + 0.1 * jax.random.normal(seeds[7], (D_TEXT,), jnp.float32), 0.5, 1.5)
    kv_weight = draw_kv_weight(jax.random.fold_in(seeds[10], 71), 0)
    lengths = ragged_sizes(seeds[9], PROMPTS, 5 * TLEN // 2, TLEN, 0).astype(jnp.int32)
    return {"queries": queries, "keys": keys, "values": values, "context": context, "residual": residual, "codes": codes, "scales": scales, "gain": gain, "kv_weight": kv_weight, "lengths": lengths}


def softmax_rows(scores):
    top = lax.optimization_barrier(jnp.max(scores, axis=-1, keepdims=True))
    weights = jnp.exp(scores - top)
    return weights / lax.optimization_barrier(jnp.sum(weights, axis=-1, keepdims=True))

def reference(queries, keys, values, context, residual, codes, scales, gain, kv_weight, lengths):
    scale_rows = jnp.repeat(scales, QGROUP, axis=0)
    weight = (codes.astype(jnp.float32) * scale_rows).astype(jnp.bfloat16)
    hidden = residual.astype(jnp.float32) + jnp.dot(context, weight, preferred_element_type=jnp.float32)
    mean_square = lax.optimization_barrier(jnp.sum(hidden * hidden, axis=1, keepdims=True)) / D_TEXT
    text = (hidden * lax.rsqrt(mean_square + 1e-06) * gain).astype(jnp.bfloat16)
    text_kv = jnp.dot(text, kv_weight, preferred_element_type=jnp.float32).astype(jnp.bfloat16)
    text_keys = text_kv[:, :D].reshape(TEXT_ROWS, HEADS, HEAD_DIM)
    text_values = text_kv[:, D:].reshape(TEXT_ROWS, HEADS, HEAD_DIM)
    factor = 1.0 / math.sqrt(HEAD_DIM)

    def self_pair(pair):
        query_rows, key_rows, value_rows = pair
        scores = jnp.dot(query_rows, key_rows.T, preferred_element_type=jnp.float32) * factor
        probs = softmax_rows(scores).astype(jnp.bfloat16)
        return jnp.dot(probs, value_rows, preferred_element_type=jnp.float32).astype(jnp.bfloat16)
    flat_shape = (SAMPLES * HEADS, LENGTH, HEAD_DIM)
    self_out = lax.map(self_pair, (queries.reshape(flat_shape), keys.reshape(flat_shape), values.reshape(flat_shape)))
    self_out = self_out.reshape(queries.shape)
    row_index = jnp.arange(TEXT_ROWS, dtype=jnp.int32)
    row_prompt = row_index // TLEN
    row_place = row_index % TLEN
    prompt_ids = jnp.arange(PROMPTS, dtype=jnp.int32)
    row_length = lax.optimization_barrier(jnp.sum(jnp.where(row_prompt[:, None] == prompt_ids[None, :], lengths[None, :], 0), axis=1))
    row_live = row_place < row_length

    def cross_one(pair):
        sample_queries, sample_index = pair
        scores = jnp.einsum('htd,rhd->htr', sample_queries.astype(jnp.float32), text_keys.astype(jnp.float32)) * factor
        allowed = row_live & (row_prompt == sample_index % PROMPTS)
        scores = jnp.where(allowed[None, None, :], scores, -1e+30)
        probs = softmax_rows(scores).astype(jnp.bfloat16)
        return jnp.einsum('htr,rhd->htd', probs.astype(jnp.float32), text_values.astype(jnp.float32))
    cross_out = lax.map(cross_one, (queries, jnp.arange(SAMPLES, dtype=jnp.int32)))
    return (self_out.astype(jnp.float32) + cross_out).astype(jnp.bfloat16)
```

```python
import math

import jax
import jax.numpy as jnp
from jax import lax
from jax.experimental import pallas as pl
from jax.experimental.pallas import tpu as pltpu
from jax.sharding import PartitionSpec as P

MESH = pl.DeviceIdType.MESH
BF16 = jnp.bfloat16
F32 = jnp.float32
FACTOR = 1.0 / math.sqrt(128)
D_TEXT = 4096


def dot_t(a, b):
    return lax.dot_general(a, b, (((1,), (1,)), ((), ())), preferred_element_type=F32)


def partner(me, i):
    z, x, y = me // 8, (me // 2) % 4, me % 2
    dz, dx, dy = (i * 3) % 8, (i // 8) % 4, (i // 32 + i) % 2
    return ((z + dz) % 8) * 8 + ((x + dx) % 4) * 2 + (y + dy) % 2


def block_of(p):
    z, x, y = p // 8, (p // 2) % 4, p % 2
    t = (z + 6) % 8
    return ((t // 4) * 4 + (x % 2) * 2 + y) * 8 + (t % 4) * 2 + x // 2


def wait_bytes(ref, sem):
    pltpu.make_async_copy(ref, ref, sem).wait()


def softmax_rows(scores):
    top = jnp.max(scores, axis=-1, keepdims=True)
    weights = jnp.exp(scores - top)
    return weights / jnp.sum(weights, axis=-1, keepdims=True)


def kernel(
    q_ref, k_ref, v_ref, context_ref, residual_ref, codes_ref, scales_ref, gain_ref, weight_ref, lengths_ref,
    out_ref,
    context, residual, codes, scales, gain, weight,
    q_all, k_all, v_all, part, sums, text, squares, rows, kv_own, kv_all, attended,
    load_sem, own_sem, send_sem, recv_sem,
):
    g = lax.axis_index("grp")
    me = lax.axis_index("seq")
    mine = block_of(me)

    barrier = pltpu.get_barrier_semaphore()

    def greet(i, carry):
        pl.semaphore_signal(barrier, inc=1, device_id={"seq": partner(me, i)}, device_id_type=MESH)
        return carry

    lax.fori_loop(1, 64, greet, 0)
    for i in range(1, 8):
        pl.semaphore_signal(barrier, inc=1, device_id={"grp": (g + i) % 8}, device_id_type=MESH)

    loads = [
        pltpu.make_async_copy(src, dst, load_sem.at[n])
        for n, (src, dst) in enumerate(
            (
                (context_ref, context),
                (codes_ref, codes),
                (scales_ref, scales),
                (residual_ref, residual),
                (gain_ref, gain),
                (weight_ref, weight),
            )
        )
    ]
    for load in loads:
        load.start()
    own = [
        pltpu.make_async_copy(src.at[mine], dst.at[:, me], own_sem.at[n])
        for n, (src, dst) in enumerate(((q_ref, q_all), (k_ref, k_all), (v_ref, v_all)))
    ]
    for copy in own:
        copy.start()
    kv_own[...] = jnp.zeros_like(kv_own)
    squares[me] = jnp.zeros((2, 128), F32)

    for load in loads[:3]:
        load.wait()
    level = jnp.concatenate([jnp.broadcast_to(scales[n : n + 1, :], (128, 64)).T for n in range(4)], axis=1)
    dense = (codes[...].astype(F32) * level).astype(BF16)
    dense = jnp.concatenate([dense, dense], axis=0)
    product = dot_t(context[...], dense).reshape(8, 2, 16, 128)
    half = lax.broadcasted_iota(jnp.int32, (16, 128), 1) // 64
    first = half == me % 2
    part[...] = jnp.where(first[None], product[:, 0], product[:, 1])
    sums[g] = part[g]

    pl.semaphore_wait(barrier, 70)

    for i in (4, 5, 3, 2, 6, 1, 7):
        to = (g + i) % 8
        pltpu.make_async_remote_copy(
            part.at[to], sums.at[g], send_sem.at[0], recv_sem.at[0], device_id={"grp": to}, device_id_type=MESH
        ).start()

    def send_tokens(i, carry):
        to = partner(me, i)
        block = block_of(to)
        for n, (src, dst) in enumerate(((k_ref, k_all), (q_ref, q_all), (v_ref, v_all))):
            pltpu.make_async_remote_copy(
                src.at[block],
                dst.at[:, me],
                send_sem.at[1 + n],
                recv_sem.at[1 + n],
                device_id={"seq": to},
                device_id_type=MESH,
            ).start()
        return carry

    lax.fori_loop(1, 64, send_tokens, 0)

    loads[3].wait()
    loads[4].wait()
    start = residual[...].astype(F32)
    start = jnp.concatenate([start, start], axis=1)
    start = jnp.where(first, start[:16], start[16:])
    wide_gain = jnp.concatenate([gain[...], gain[...]], axis=1)
    wait_bytes(sums.at[0:7], recv_sem.at[0])
    hidden = start + jnp.sum(sums[...], axis=0)
    text[me] = (hidden * wide_gain).astype(BF16)
    pick = (lax.broadcasted_iota(jnp.int32, (2, 128), 0) == (lax.broadcasted_iota(jnp.int32, (2, 128), 1) // 64 + me) % 2)
    squares[me, :, 0:16] = lax.dot_general(
        pick.astype(F32),
        hidden * hidden,
        (((1,), (1,)), ((), ())),
        preferred_element_type=F32,
        precision=lax.Precision.HIGHEST,
    )

    def send_text(i, carry):
        to = partner(me, i)
        for n, buf in enumerate((text, squares)):
            pltpu.make_async_remote_copy(
                buf.at[me],
                buf.at[me],
                send_sem.at[4 + n],
                recv_sem.at[4 + n],
                device_id={"seq": to},
                device_id_type=MESH,
            ).start()
        return carry

    lax.fori_loop(1, 64, send_text, 0)

    wait_bytes(squares.at[0:63], recv_sem.at[5])
    norm = lax.rsqrt(jnp.sum(squares[...], axis=0) / D_TEXT + 1e-06)
    diagonal = lax.broadcasted_iota(jnp.int32, (16, 128), 0) == lax.broadcasted_iota(jnp.int32, (16, 128), 1)
    norm = jnp.concatenate(
        [jnp.sum(jnp.where(diagonal, norm[n : n + 1], 0.0), axis=1, keepdims=True) for n in range(2)], axis=0
    )
    wait_bytes(text.at[0:63], recv_sem.at[4])
    pairs = text[...].reshape(32, 2, 16, 128)
    even, odd = pairs[:, 0], pairs[:, 1]
    left = (half == 0)[None]
    upper = jnp.where(left, even, odd)
    lower = jnp.where(left, odd, even).astype(F32).reshape(512, 128)
    lower = pltpu.roll(lower, 64, 1).reshape(32, 16, 128).astype(BF16)
    for n in range(32):
        rows[0:16, 128 * n : 128 * n + 128] = upper[n]
        rows[16:32, 128 * n : 128 * n + 128] = lower[n]
    loads[5].wait()
    kv_own[:, 0:96] = (dot_t(rows[...], weight[...]) * norm).astype(BF16)

    prompt, triple = g // 2, (me % 32) // 4
    slot = (me // 32) * 4 + me % 4

    def send_kv(i, carry):
        z = (triple // 2 + 2 + 4 * (i % 2)) % 8
        x = (triple % 2) * 2 + prompt // 2
        pltpu.make_async_remote_copy(
            kv_own,
            kv_all.at[slot, g % 2],
            send_sem.at[6],
            recv_sem.at[6],
            device_id={"grp": (g + i // 2) % 8, "seq": z * 8 + x * 2 + prompt % 2},
            device_id_type=MESH,
        ).start()
        return carry

    lax.fori_loop(0, 16, send_kv, 0)

    for copy in own:
        copy.wait()
    for n in range(3):
        wait_bytes(q_ref.at[0:63], recv_sem.at[1 + n])
    self_out = []
    for n in range(3):
        scores = dot_t(q_all[n].reshape(256, 128), k_all[n].reshape(256, 128)) * FACTOR
        probs = softmax_rows(scores).astype(BF16)
        self_out.append(jnp.dot(probs, v_all[n].reshape(256, 128), preferred_element_type=F32).astype(BF16))

    length = lengths_ref[(mine // 8) % 4]
    live = lax.broadcasted_iota(jnp.int32, (256, 64), 1) < length
    source = lax.broadcasted_iota(jnp.int32, (128, 384), 0)
    target = lax.broadcasted_iota(jnp.int32, (128, 384), 1)
    wait_bytes(kv_all, recv_sem.at[6])
    text_keys = jnp.zeros((64, 384), F32)
    text_values = jnp.zeros((64, 384), F32)
    for n in range(4):
        place = ((source + 96 * n == target) & (source < 96)).astype(BF16)
        text_keys += jnp.dot(kv_all[n].reshape(64, 128), place, preferred_element_type=F32)
        text_values += jnp.dot(kv_all[4 + n].reshape(64, 128), place, preferred_element_type=F32)
    text_keys, text_values = text_keys.astype(BF16), text_values.astype(BF16)
    for n in range(3):
        columns = slice(128 * n, 128 * n + 128)
        scores = dot_t(q_all[n].reshape(256, 128), text_keys[:, columns]) * FACTOR
        probs = softmax_rows(jnp.where(live, scores, -1e30)).astype(BF16)
        cross = jnp.dot(probs, text_values[:, columns], preferred_element_type=F32)
        attended[n] = (self_out[n].astype(F32) + cross).astype(BF16).reshape(64, 4, 128)

    def send_out(i, carry):
        to = partner(me, i)
        pltpu.make_async_remote_copy(
            attended.at[:, to],
            out_ref.at[mine],
            send_sem.at[7],
            recv_sem.at[7],
            device_id={"seq": to},
            device_id_type=MESH,
        ).start()
        return carry

    lax.fori_loop(1, 64, send_out, 0)
    last = pltpu.make_async_copy(attended.at[:, me], out_ref.at[mine], own_sem.at[3])
    last.start()

    wait_bytes(part.at[0:7], send_sem.at[0])
    for n in range(3):
        wait_bytes(q_ref.at[0:63], send_sem.at[1 + n])
    wait_bytes(text.at[0:63], send_sem.at[4])
    wait_bytes(squares.at[0:63], send_sem.at[5])
    wait_bytes(kv_all, send_sem.at[6])
    last.wait()
    wait_bytes(q_ref.at[0:63], send_sem.at[7])
    wait_bytes(q_ref.at[0:63], recv_sem.at[7])


def local(queries, keys, values, context, residual, codes, scales, gain, kv_weight, lengths):
    blocks = (64, 3, 4, 128)
    anywhere = pl.BlockSpec(memory_space=pl.ANY)
    tokens = pltpu.VMEM((3, 64, 4, 128), BF16)
    out = pl.pallas_call(
        kernel,
        out_shape=jax.ShapeDtypeStruct(blocks, BF16),
        in_specs=[anywhere] * 9 + [pl.BlockSpec(memory_space=pltpu.SMEM)],
        out_specs=anywhere,
        scratch_shapes=[
            pltpu.VMEM((256, 512), BF16),
            pltpu.VMEM((32, 64), BF16),
            pltpu.VMEM((64, 512), jnp.int32),
            pltpu.VMEM((4, 64), F32),
            pltpu.VMEM((1, 64), F32),
            pltpu.VMEM((96, 4096), BF16),
            tokens,
            tokens,
            tokens,
            pltpu.VMEM((8, 16, 128), F32),
            pltpu.VMEM((8, 16, 128), F32),
            pltpu.VMEM((64, 16, 128), BF16),
            pltpu.VMEM((64, 2, 128), F32),
            pltpu.VMEM((32, 4096), BF16),
            pltpu.VMEM((32, 128), BF16),
            pltpu.VMEM((8, 2, 32, 128), BF16),
            tokens,
            pltpu.SemaphoreType.DMA((6,)),
            pltpu.SemaphoreType.DMA((4,)),
            pltpu.SemaphoreType.DMA((8,)),
            pltpu.SemaphoreType.DMA((8,)),
        ],
        compiler_params=pltpu.CompilerParams(
            collective_id=0, has_side_effects=True, vmem_limit_bytes=32 * 1024 * 1024
        ),
        name="block",
    )(
        queries.reshape(blocks),
        keys.reshape(blocks),
        values.reshape(blocks),
        context,
        residual,
        codes.T,
        scales,
        gain.reshape(1, 64),
        kv_weight.T,
        lengths,
    )
    return out.reshape(queries.shape)


def solution(mesh):
    placed = (
        P("grp", None, "seq", None),
        P("grp", None, "seq", None),
        P("grp", None, "seq", None),
        P(None, "grp"),
        P("grp", "seq"),
        P("grp", "seq"),
        P("grp", "seq"),
        P("seq"),
        P(None, "seq"),
        P(),
    )
    return jax.shard_map(
        local, mesh=mesh, in_specs=placed, out_specs=P("grp", None, "seq", None), check_vma=False
    )
```

```python
import math

import jax
import jax.numpy as jnp
from jax import lax
from jax.experimental import pallas as pl
from jax.experimental.pallas import tpu as pltpu
from jax.sharding import PartitionSpec as P

MESH = pl.DeviceIdType.MESH
BF16 = jnp.bfloat16
F32 = jnp.float32
FACTOR = 1.0 / math.sqrt(128)
D_TEXT = 4096


def dot_t(a, b):
    return lax.dot_general(a, b, (((1,), (1,)), ((), ())), preferred_element_type=F32)


def partner(me, dz, dxy):
    z, x, y = me // 8, (me // 2) % 4, me % 2
    return ((z + dz) % 8) * 8 + ((x + dxy // 2) % 4) * 2 + (y + dxy) % 2


def block_of(p):
    z, x, y = p // 8, (p // 2) % 4, p % 2
    t = (z + 6) % 8
    return ((t // 4) * 4 + (x % 2) * 2 + y) * 8 + (t % 4) * 2 + x // 2


def wait_bytes(ref, sem):
    pltpu.make_async_copy(ref, ref, sem).wait()


def softmax_rows(scores):
    top = jnp.max(scores, axis=-1, keepdims=True)
    weights = jnp.exp(scores - top)
    return weights / jnp.sum(weights, axis=-1, keepdims=True)


def kernel(
    q_ref, k_ref, v_ref, context_ref, residual_ref, codes_ref, scales_ref, gain_ref, weight_ref, lengths_ref,
    out_ref,
    context, residual, codes, scales, gain, weight,
    q_all, k_all, v_all, part, sums, text, squares_z, squares, rows, kv_own, kv_all, attended,
    load_sem, own_sem, send_sem, recv_sem, ready_sem,
):
    g = lax.axis_index("grp")
    me = lax.axis_index("seq")
    z, xy = me // 8, me % 8
    mine = block_of(me)

    barrier = pltpu.get_barrier_semaphore()
    for i in (4, 5, 3, 2, 6, 1, 7):
        pl.semaphore_signal(barrier, inc=1, device_id={"grp": (g + i) % 8}, device_id_type=MESH)
        pl.semaphore_signal(barrier, inc=1, device_id={"seq": partner(me, i, 0)}, device_id_type=MESH)
        pl.semaphore_signal(barrier, inc=1, device_id={"seq": partner(me, 0, i)}, device_id_type=MESH)

    loads = [
        pltpu.make_async_copy(src, dst, load_sem.at[n])
        for n, (src, dst) in enumerate(
            (
                (codes_ref, codes),
                (scales_ref, scales),
                (context_ref, context),
                (residual_ref, residual),
                (gain_ref, gain),
                (weight_ref, weight),
            )
        )
    ]
    for load in loads:
        load.start()
    arrays = ((k_ref, k_all), (q_ref, q_all), (v_ref, v_all))
    own = [pltpu.make_async_copy(src.at[mine], dst.at[:, me], own_sem.at[n]) for n, (src, dst) in enumerate(arrays)]
    for copy in own:
        copy.start()
    kv_own[...] = jnp.zeros_like(kv_own)
    squares_z[z] = jnp.zeros((2, 128), F32)

    for load in loads[:3]:
        load.wait()
    level = jnp.concatenate([jnp.broadcast_to(scales[n : n + 1, :], (128, 64)).T for n in range(4)], axis=1)
    dense = (codes[...].astype(F32) * level).astype(BF16)
    dense = jnp.concatenate([dense, dense], axis=0)
    product = dot_t(context[...], dense).reshape(8, 2, 16, 128)
    half = lax.broadcasted_iota(jnp.int32, (16, 128), 1) // 64
    first = half == me % 2
    part[...] = jnp.where(first[None], product[:, 0], product[:, 1])
    sums[g] = part[g]

    pl.semaphore_wait(barrier, 21)

    for i in (4, 5, 3, 2, 6, 1, 7):
        to = (g + i) % 8
        pltpu.make_async_remote_copy(
            part.at[to], sums.at[g], send_sem.at[0], recv_sem.at[0], device_id={"grp": to}, device_id_type=MESH
        ).start()
    for i in (4, 3, 5, 2, 6, 1, 7):
        pl.semaphore_signal(ready_sem, inc=1, device_id={"seq": partner(me, i, 0)}, device_id_type=MESH)

    def send_tokens(n, to):
        src, dst = arrays[n]
        pltpu.make_async_remote_copy(
            src.at[block_of(to)],
            dst.at[:, me],
            send_sem.at[1 + n],
            recv_sem.at[1 + n],
            device_id={"seq": to},
            device_id_type=MESH,
        ).start()

    def send_near(n):
        for i in (4, 3, 5, 2, 6, 1, 7):
            send_tokens(n, partner(me, i, 0))
            send_tokens(n, partner(me, 0, i))

    def send_far(n):
        def step(i, carry):
            send_tokens(n, partner(me, 1 + (i * 3) % 7, 1 + i // 7))
            return carry

        lax.fori_loop(0, 49, step, 0)

    for n in (0, 1, 2):
        send_near(n)

    loads[3].wait()
    loads[4].wait()
    start = residual[...].astype(F32)
    start = jnp.concatenate([start, start], axis=1)
    start = jnp.where(first, start[:16], start[16:])
    wide_gain = jnp.concatenate([gain[...], gain[...]], axis=1)
    pl.semaphore_wait(ready_sem, 7)
    for n in (0,):
        send_far(n)
    wait_bytes(sums.at[0:7], recv_sem.at[0])
    hidden = start + jnp.sum(sums[...], axis=0)
    text[xy, z] = (hidden * wide_gain).astype(BF16)
    pick = lax.broadcasted_iota(jnp.int32, (2, 128), 0) == (lax.broadcasted_iota(jnp.int32, (2, 128), 1) // 64 + me) % 2
    squares_z[z, :, 0:16] = lax.dot_general(
        pick.astype(F32),
        hidden * hidden,
        (((1,), (1,)), ((), ())),
        preferred_element_type=F32,
        precision=lax.Precision.HIGHEST,
    )

    def send_line(buf, at, n, to):
        pltpu.make_async_remote_copy(
            buf.at[at], buf.at[at], send_sem.at[n], recv_sem.at[n], device_id={"seq": to}, device_id_type=MESH
        ).start()

    for i in (4, 3, 5, 2, 6, 1, 7):
        send_line(text, (xy, z), 10 + z, partner(me, i, 0))

    def forward(plane):
        @pl.when(plane != z)
        def _():
            wait_bytes(text.at[0, 0], recv_sem.at[10 + plane])

        for i in (5, 4, 7, 6, 3, 2, 1):
            send_line(text, (xy, plane), 6, partner(me, 0, i))

    for i in (4, 3, 5, 2, 6, 1, 7):
        send_line(squares_z, z, 5, partner(me, i, 0))
    for n in (1,):
        send_far(n)

    def forward_one(i, carry):
        forward(i)
        return carry

    lax.fori_loop(0, 8, forward_one, 0)
    wait_bytes(squares_z.at[0:7], recv_sem.at[5])
    squares[xy] = jnp.sum(squares_z[...], axis=0)
    for i in (5, 4, 7, 6, 3, 2, 1):
        send_line(squares, xy, 7, partner(me, 0, i))
    for n in (2,):
        send_far(n)

    wait_bytes(squares.at[0:7], recv_sem.at[7])
    norm = lax.rsqrt(jnp.sum(squares[...], axis=0) / D_TEXT + 1e-06)
    diagonal = lax.broadcasted_iota(jnp.int32, (16, 128), 0) == lax.broadcasted_iota(jnp.int32, (16, 128), 1)
    norm = jnp.concatenate(
        [jnp.sum(jnp.where(diagonal, norm[n : n + 1], 0.0), axis=1, keepdims=True) for n in range(2)], axis=0
    )
    wait_bytes(text.at[0:7], recv_sem.at[6])
    left = (half == 0)[None]
    for x in range(4):
        even, odd = text[2 * x], text[2 * x + 1]
        upper = jnp.where(left, even, odd)
        lower = jnp.where(left, odd, even).astype(F32).reshape(128, 128)
        lower = pltpu.roll(lower, 64, 1).reshape(8, 16, 128).astype(BF16)
        for n in range(8):
            at = 128 * (4 * n + x)
            rows[0:16, at : at + 128] = upper[n]
            rows[16:32, at : at + 128] = lower[n]
    loads[5].wait()
    kv_own[:, 0:96] = (dot_t(rows[...], weight[...]) * norm).astype(BF16)

    prompt, triple = g // 2, (me % 32) // 4
    slot = (me // 32) * 4 + me % 4

    def send_kv(i, carry):
        to_z = (triple // 2 + 2 + 4 * (i % 2)) % 8
        to_x = (triple % 2) * 2 + prompt // 2
        pltpu.make_async_remote_copy(
            kv_own,
            kv_all.at[slot, g % 2],
            send_sem.at[8],
            recv_sem.at[8],
            device_id={"grp": (g + 4 + i // 2) % 8, "seq": to_z * 8 + to_x * 2 + prompt % 2},
            device_id_type=MESH,
        ).start()
        return carry

    lax.fori_loop(0, 16, send_kv, 0)
    for n in ():
        send_far(n)

    for copy in own:
        copy.wait()
    for n in range(3):
        wait_bytes(q_ref.at[0:63], recv_sem.at[1 + n])
    self_out = []
    for n in range(3):
        scores = dot_t(q_all[n].reshape(256, 128), k_all[n].reshape(256, 128)) * FACTOR
        probs = softmax_rows(scores).astype(BF16)
        self_out.append(jnp.dot(probs, v_all[n].reshape(256, 128), preferred_element_type=F32).astype(BF16))

    length = lengths_ref[(mine // 8) % 4]
    live = lax.broadcasted_iota(jnp.int32, (256, 64), 1) < length
    source = lax.broadcasted_iota(jnp.int32, (128, 384), 0)
    target = lax.broadcasted_iota(jnp.int32, (128, 384), 1)
    places = [((source + 96 * n == target) & (source < 96)).astype(BF16) for n in range(4)]
    wait_bytes(kv_all, recv_sem.at[8])
    text_keys = jnp.zeros((64, 384), F32)
    text_values = jnp.zeros((64, 384), F32)
    for n in range(4):
        text_keys += jnp.dot(kv_all[n].reshape(64, 128), places[n], preferred_element_type=F32)
        text_values += jnp.dot(kv_all[4 + n].reshape(64, 128), places[n], preferred_element_type=F32)
    text_keys, text_values = text_keys.astype(BF16), text_values.astype(BF16)
    for n in range(3):
        columns = slice(128 * n, 128 * n + 128)
        scores = dot_t(q_all[n].reshape(256, 128), text_keys[:, columns]) * FACTOR
        probs = softmax_rows(jnp.where(live, scores, -1e30)).astype(BF16)
        cross = jnp.dot(probs, text_values[:, columns], preferred_element_type=F32)
        attended[n] = (self_out[n].astype(F32) + cross).astype(BF16).reshape(64, 4, 128)

    def send_out(i, carry):
        to_z = i // 8
        to = to_z * 8 + ((xy // 2 + (i % 8) // 2) % 4) * 2 + (xy + i) % 2
        pltpu.make_async_remote_copy(
            attended.at[:, to],
            out_ref.at[mine],
            send_sem.at[9],
            recv_sem.at[9],
            device_id={"seq": to},
            device_id_type=MESH,
        ).start()
        return carry

    lax.fori_loop(0, z * 8, send_out, 0)
    lax.fori_loop(z * 8 + 1, 64, send_out, 0)
    last = pltpu.make_async_copy(attended.at[:, me], out_ref.at[mine], own_sem.at[3])
    last.start()

    wait_bytes(part.at[0:7], send_sem.at[0])
    for n in range(3):
        wait_bytes(q_ref.at[0:63], send_sem.at[1 + n])
    wait_bytes(text.at[0, 0:7], send_sem.at[10 + z])
    wait_bytes(squares_z.at[0:7], send_sem.at[5])
    wait_bytes(text.at[0:7], send_sem.at[6])
    wait_bytes(squares.at[0:7], send_sem.at[7])
    wait_bytes(kv_all, send_sem.at[8])
    last.wait()
    wait_bytes(q_ref.at[0:63], send_sem.at[9])
    wait_bytes(q_ref.at[0:63], recv_sem.at[9])


def local(queries, keys, values, context, residual, codes, scales, gain, kv_weight, lengths):
    blocks = (64, 3, 4, 128)
    anywhere = pl.BlockSpec(memory_space=pl.ANY)
    tokens = pltpu.VMEM((3, 64, 4, 128), BF16)
    out = pl.pallas_call(
        kernel,
        out_shape=pltpu.VMEM(blocks, BF16),
        in_specs=[anywhere] * 9 + [pl.BlockSpec(memory_space=pltpu.SMEM)],
        out_specs=pl.BlockSpec(memory_space=pltpu.VMEM),
        scratch_shapes=[
            pltpu.VMEM((256, 512), BF16),
            pltpu.VMEM((32, 64), BF16),
            pltpu.VMEM((64, 512), jnp.int32),
            pltpu.VMEM((4, 64), F32),
            pltpu.VMEM((1, 64), F32),
            pltpu.VMEM((96, 4096), BF16),
            tokens,
            tokens,
            tokens,
            pltpu.VMEM((8, 16, 128), F32),
            pltpu.VMEM((8, 16, 128), F32),
            pltpu.VMEM((8, 8, 16, 128), BF16),
            pltpu.VMEM((8, 2, 128), F32),
            pltpu.VMEM((8, 2, 128), F32),
            pltpu.VMEM((32, 4096), BF16),
            pltpu.VMEM((32, 128), BF16),
            pltpu.VMEM((8, 2, 32, 128), BF16),
            tokens,
            pltpu.SemaphoreType.DMA((6,)),
            pltpu.SemaphoreType.DMA((4,)),
            pltpu.SemaphoreType.DMA((18,)),
            pltpu.SemaphoreType.DMA((18,)),
            pltpu.SemaphoreType.REGULAR,
        ],
        compiler_params=pltpu.CompilerParams(
            collective_id=0, has_side_effects=True, vmem_limit_bytes=60 * 1024 * 1024
        ),
        name="block",
    )(
        queries.reshape(blocks),
        keys.reshape(blocks),
        values.reshape(blocks),
        context,
        residual,
        codes.T,
        scales,
        gain.reshape(1, 64),
        kv_weight.T,
        lengths,
    )
    return out.reshape(queries.shape)


def solution(mesh):
    placed = (
        P("grp", None, "seq", None),
        P("grp", None, "seq", None),
        P("grp", None, "seq", None),
        P(None, "grp"),
        P("grp", "seq"),
        P("grp", "seq"),
        P("grp", "seq"),
        P("seq"),
        P(None, "seq"),
        P(),
    )
    return jax.shard_map(
        local, mesh=mesh, in_specs=placed, out_specs=P("grp", None, "seq", None), check_vma=False
    )
```

```python
import math

import jax
import jax.numpy as jnp
from jax import lax
from jax.experimental import pallas as pl
from jax.experimental.pallas import tpu as pltpu
from jax.sharding import PartitionSpec as P

MESH = pl.DeviceIdType.MESH
BF16 = jnp.bfloat16
F32 = jnp.float32
FACTOR = 1.0 / math.sqrt(128)
D_TEXT = 4096


def dot_t(a, b):
    return lax.dot_general(a, b, (((1,), (1,)), ((), ())), preferred_element_type=F32)


def partner(me, dz, dxy):
    z, x, y = me // 8, (me // 2) % 4, me % 2
    return ((z + dz) % 8) * 8 + ((x + dxy // 2) % 4) * 2 + (y + dxy) % 2


def block_of(p):
    z, x, y = p // 8, (p // 2) % 4, p % 2
    t = (z + 6) % 8
    return ((t // 4) * 4 + (x % 2) * 2 + y) * 8 + (t % 4) * 2 + x // 2


def wait_bytes(ref, sem):
    pltpu.make_async_copy(ref, ref, sem).wait()


def softmax_rows(scores):
    top = jnp.max(scores, axis=-1, keepdims=True)
    weights = jnp.exp(scores - top)
    return weights / jnp.sum(weights, axis=-1, keepdims=True)


def kernel(
    q_ref, k_ref, v_ref, context_ref, residual_ref, codes_ref, scales_ref, gain_ref, weight_ref, lengths_ref,
    out_ref,
    context, residual, codes, scales, gain, weight,
    q_all, k_all, v_all, part, sums, text, squares_z, squares, rows, kv_own, kv_all, attended,
    load_sem, own_sem, send_sem, recv_sem, ready_sem,
):
    g = lax.axis_index("grp")
    me = lax.axis_index("seq")
    z, xy = me // 8, me % 8
    mine = block_of(me)

    barrier = pltpu.get_barrier_semaphore()
    for i in (4, 5, 3, 2, 6, 1, 7):
        pl.semaphore_signal(barrier, inc=1, device_id={"grp": (g + i) % 8}, device_id_type=MESH)
        pl.semaphore_signal(barrier, inc=1, device_id={"seq": partner(me, i, 0)}, device_id_type=MESH)
        pl.semaphore_signal(barrier, inc=1, device_id={"seq": partner(me, 0, i)}, device_id_type=MESH)

    loads = [
        pltpu.make_async_copy(src, dst, load_sem.at[n])
        for n, (src, dst) in enumerate(
            (
                (codes_ref, codes),
                (scales_ref, scales),
                (context_ref, context),
                (residual_ref, residual),
                (gain_ref, gain),
                (weight_ref, weight),
            )
        )
    ]
    for load in loads:
        load.start()
    arrays = ((k_ref, k_all), (q_ref, q_all), (v_ref, v_all))
    own = [pltpu.make_async_copy(src.at[mine], dst.at[:, me], own_sem.at[n]) for n, (src, dst) in enumerate(arrays)]
    for copy in own:
        copy.start()
    kv_own[...] = jnp.zeros_like(kv_own)
    squares_z[z] = jnp.zeros((2, 128), F32)

    for load in loads[:3]:
        load.wait()
    level = jnp.concatenate([jnp.broadcast_to(scales[n : n + 1, :], (128, 64)).T for n in range(4)], axis=1)
    dense = (codes[...].astype(F32) * level).astype(BF16)
    dense = jnp.concatenate([dense, dense], axis=0)
    product = dot_t(context[...], dense).reshape(8, 2, 16, 128)
    half = lax.broadcasted_iota(jnp.int32, (16, 128), 1) // 64
    first = half == me % 2
    part[...] = jnp.where(first[None], product[:, 0], product[:, 1])
    sums[g] = part[g]

    pl.semaphore_wait(barrier, 21)

    for i in (4, 5, 3, 2, 6, 1, 7):
        to = (g + i) % 8
        pltpu.make_async_remote_copy(
            part.at[to], sums.at[g], send_sem.at[0], recv_sem.at[0], device_id={"grp": to}, device_id_type=MESH
        ).start()
    for i in (4, 3, 5, 2, 6, 1, 7):
        pl.semaphore_signal(ready_sem, inc=1, device_id={"seq": partner(me, i, 0)}, device_id_type=MESH)

    def send_tokens(n, to):
        src, dst = arrays[n]
        pltpu.make_async_remote_copy(
            src.at[block_of(to)],
            dst.at[:, me],
            send_sem.at[1 + n],
            recv_sem.at[1 + n],
            device_id={"seq": to},
            device_id_type=MESH,
        ).start()

    def send_near(n):
        for i in (4, 3, 5, 2, 6, 1, 7):
            send_tokens(n, partner(me, i, 0))
            send_tokens(n, partner(me, 0, i))

    def send_part(n, low, high):
        def step(i, carry):
            send_tokens(n, partner(me, 1 + (i * 3) % 7, 1 + i // 7))
            return carry

        lax.fori_loop(low, high, step, 0)

    for n in range(3):
        send_near(n)

    loads[3].wait()
    loads[4].wait()
    start = residual[...].astype(F32)
    start = jnp.concatenate([start, start], axis=1)
    start = jnp.where(first, start[:16], start[16:])
    wide_gain = jnp.concatenate([gain[...], gain[...]], axis=1)
    pl.semaphore_wait(ready_sem, 7)
    send_part(0, 0, 28)
    wait_bytes(sums.at[0:7], recv_sem.at[0])
    hidden = start + jnp.sum(sums[...], axis=0)
    text[xy, z] = (hidden * wide_gain).astype(BF16)
    pick = lax.broadcasted_iota(jnp.int32, (2, 128), 0) == (lax.broadcasted_iota(jnp.int32, (2, 128), 1) // 64 + me) % 2
    squares_z[z, :, 0:16] = lax.dot_general(
        pick.astype(F32),
        hidden * hidden,
        (((1,), (1,)), ((), ())),
        preferred_element_type=F32,
        precision=lax.Precision.HIGHEST,
    )

    def send_line(buf, at, n, to):
        pltpu.make_async_remote_copy(
            buf.at[at], buf.at[at], send_sem.at[n], recv_sem.at[n], device_id={"seq": to}, device_id_type=MESH
        ).start()

    for i in (4, 3, 5, 2, 6, 1, 7):
        send_line(text, (xy, z), 10 + z, partner(me, i, 0))

    def forward(plane):
        @pl.when(plane != z)
        def _():
            wait_bytes(text.at[0, 0], recv_sem.at[10 + plane])

        for i in (5, 4, 7, 6, 3, 2, 1):
            send_line(text, (xy, plane), 6, partner(me, 0, i))

    for i in (4, 3, 5, 2, 6, 1, 7):
        send_line(squares_z, z, 5, partner(me, i, 0))

    send_part(0, 28, 49)
    send_part(1, 0, 35)

    def forward_one(i, carry):
        forward(i)
        return carry

    lax.fori_loop(0, 8, forward_one, 0)
    wait_bytes(squares_z.at[0:7], recv_sem.at[5])
    squares[xy] = jnp.sum(squares_z[...], axis=0)
    for i in (5, 4, 7, 6, 3, 2, 1):
        send_line(squares, xy, 7, partner(me, 0, i))
    send_part(1, 35, 49)
    send_part(2, 0, 49)

    wait_bytes(squares.at[0:7], recv_sem.at[7])
    norm = lax.rsqrt(jnp.sum(squares[...], axis=0) / D_TEXT + 1e-06)
    diagonal = lax.broadcasted_iota(jnp.int32, (16, 128), 0) == lax.broadcasted_iota(jnp.int32, (16, 128), 1)
    norm = jnp.concatenate(
        [jnp.sum(jnp.where(diagonal, norm[n : n + 1], 0.0), axis=1, keepdims=True) for n in range(2)], axis=0
    )
    wait_bytes(text.at[0:7], recv_sem.at[6])
    left = (half == 0)[None]
    for x in range(4):
        even, odd = text[2 * x], text[2 * x + 1]
        upper = jnp.where(left, even, odd)
        lower = jnp.where(left, odd, even).astype(F32).reshape(128, 128)
        lower = pltpu.roll(lower, 64, 1).reshape(8, 16, 128).astype(BF16)
        for n in range(8):
            at = 128 * (4 * n + x)
            rows[0:16, at : at + 128] = upper[n]
            rows[16:32, at : at + 128] = lower[n]
    loads[5].wait()
    kv_own[:, 0:96] = (dot_t(rows[...], weight[...]) * norm).astype(BF16)

    prompt, triple = g // 2, (me % 32) // 4
    slot = (me // 32) * 4 + me % 4

    def send_kv(i, carry):
        to_z = (triple // 2 + 2 + 4 * (i % 2)) % 8
        to_x = (triple % 2) * 2 + prompt // 2
        pltpu.make_async_remote_copy(
            kv_own,
            kv_all.at[slot, g % 2],
            send_sem.at[8],
            recv_sem.at[8],
            device_id={"grp": i // 2, "seq": to_z * 8 + to_x * 2 + prompt % 2},
            device_id_type=MESH,
        ).start()
        return carry

    lax.fori_loop(0, 16, send_kv, 0)

    for copy in own:
        copy.wait()
    for n in range(3):
        wait_bytes(q_ref.at[0:63], recv_sem.at[1 + n])
    self_out = []
    for n in range(3):
        scores = dot_t(q_all[n].reshape(256, 128), k_all[n].reshape(256, 128)) * FACTOR
        probs = softmax_rows(scores).astype(BF16)
        self_out.append(jnp.dot(probs, v_all[n].reshape(256, 128), preferred_element_type=F32).astype(BF16))

    length = lengths_ref[(mine // 8) % 4]
    live = lax.broadcasted_iota(jnp.int32, (256, 64), 1) < length
    source = lax.broadcasted_iota(jnp.int32, (128, 384), 0)
    target = lax.broadcasted_iota(jnp.int32, (128, 384), 1)
    places = [((source + 96 * n == target) & (source < 96)).astype(BF16) for n in range(4)]
    wait_bytes(kv_all, recv_sem.at[8])
    text_keys = jnp.zeros((64, 384), F32)
    text_values = jnp.zeros((64, 384), F32)
    for n in range(4):
        text_keys += jnp.dot(kv_all[n].reshape(64, 128), places[n], preferred_element_type=F32)
        text_values += jnp.dot(kv_all[4 + n].reshape(64, 128), places[n], preferred_element_type=F32)
    text_keys, text_values = text_keys.astype(BF16), text_values.astype(BF16)
    for n in range(3):
        columns = slice(128 * n, 128 * n + 128)
        scores = dot_t(q_all[n].reshape(256, 128), text_keys[:, columns]) * FACTOR
        probs = softmax_rows(jnp.where(live, scores, -1e30)).astype(BF16)
        cross = jnp.dot(probs, text_values[:, columns], preferred_element_type=F32)
        attended[n] = (self_out[n].astype(F32) + cross).astype(BF16).reshape(64, 4, 128)

    def send_out(i, carry):
        to_z = i // 8
        to = to_z * 8 + ((xy // 2 + (i % 8) // 2) % 4) * 2 + (xy + i) % 2
        pltpu.make_async_remote_copy(
            attended.at[:, to],
            out_ref.at[mine],
            send_sem.at[9],
            recv_sem.at[9],
            device_id={"seq": to},
            device_id_type=MESH,
        ).start()
        return carry

    lax.fori_loop(0, z * 8, send_out, 0)
    lax.fori_loop(z * 8 + 1, 64, send_out, 0)
    last = pltpu.make_async_copy(attended.at[:, me], out_ref.at[mine], own_sem.at[3])
    last.start()

    wait_bytes(part.at[0:7], send_sem.at[0])
    for n in range(3):
        wait_bytes(q_ref.at[0:63], send_sem.at[1 + n])
    wait_bytes(text.at[0, 0:7], send_sem.at[10 + z])
    wait_bytes(squares_z.at[0:7], send_sem.at[5])
    wait_bytes(text.at[0:7], send_sem.at[6])
    wait_bytes(squares.at[0:7], send_sem.at[7])
    wait_bytes(kv_all, send_sem.at[8])
    last.wait()
    wait_bytes(q_ref.at[0:63], send_sem.at[9])
    wait_bytes(q_ref.at[0:63], recv_sem.at[9])


def local(queries, keys, values, context, residual, codes, scales, gain, kv_weight, lengths):
    blocks = (64, 3, 4, 128)
    anywhere = pl.BlockSpec(memory_space=pl.ANY)
    tokens = pltpu.VMEM((3, 64, 4, 128), BF16)
    out = pl.pallas_call(
        kernel,
        out_shape=pltpu.VMEM(blocks, BF16),
        in_specs=[anywhere] * 9 + [pl.BlockSpec(memory_space=pltpu.SMEM)],
        out_specs=pl.BlockSpec(memory_space=pltpu.VMEM),
        scratch_shapes=[
            pltpu.VMEM((256, 512), BF16),
            pltpu.VMEM((32, 64), BF16),
            pltpu.VMEM((64, 512), jnp.int32),
            pltpu.VMEM((4, 64), F32),
            pltpu.VMEM((1, 64), F32),
            pltpu.VMEM((96, 4096), BF16),
            tokens,
            tokens,
            tokens,
            pltpu.VMEM((8, 16, 128), F32),
            pltpu.VMEM((8, 16, 128), F32),
            pltpu.VMEM((8, 8, 16, 128), BF16),
            pltpu.VMEM((8, 2, 128), F32),
            pltpu.VMEM((8, 2, 128), F32),
            pltpu.VMEM((32, 4096), BF16),
            pltpu.VMEM((32, 128), BF16),
            pltpu.VMEM((8, 2, 32, 128), BF16),
            tokens,
            pltpu.SemaphoreType.DMA((6,)),
            pltpu.SemaphoreType.DMA((4,)),
            pltpu.SemaphoreType.DMA((18,)),
            pltpu.SemaphoreType.DMA((18,)),
            pltpu.SemaphoreType.REGULAR,
        ],
        compiler_params=pltpu.CompilerParams(
            collective_id=0, has_side_effects=True, vmem_limit_bytes=60 * 1024 * 1024
        ),
        name="block",
    )(
        queries.reshape(blocks),
        keys.reshape(blocks),
        values.reshape(blocks),
        context,
        residual,
        codes.T,
        scales,
        gain.reshape(1, 64),
        kv_weight.T,
        lengths,
    )
    return out.reshape(queries.shape)


def solution(mesh):
    placed = (
        P("grp", None, "seq", None),
        P("grp", None, "seq", None),
        P("grp", None, "seq", None),
        P(None, "grp"),
        P("grp", "seq"),
        P("grp", "seq"),
        P("grp", "seq"),
        P("seq"),
        P(None, "seq"),
        P(),
    )
    return jax.shard_map(
        local, mesh=mesh, in_specs=placed, out_specs=P("grp", None, "seq", None), check_vma=False
    )
```

```python
import math

import jax
import jax.numpy as jnp
from jax import lax
from jax.experimental import pallas as pl
from jax.experimental.pallas import tpu as pltpu
from jax.sharding import PartitionSpec as P

MESH = pl.DeviceIdType.MESH
BF16 = jnp.bfloat16
F32 = jnp.float32
FACTOR = 1.0 / math.sqrt(128)
D_TEXT = 4096


def dot_t(a, b):
    return lax.dot_general(a, b, (((1,), (1,)), ((), ())), preferred_element_type=F32)


def partner(me, dz, dxy):
    z, x, y = me // 8, (me // 2) % 4, me % 2
    return ((z + dz) % 8) * 8 + ((x + dxy // 2) % 4) * 2 + (y + dxy) % 2


def block_of(p):
    z, x, y = p // 8, (p // 2) % 4, p % 2
    t = (z + 6) % 8
    return ((t // 4) * 4 + (x % 2) * 2 + y) * 8 + (t % 4) * 2 + x // 2


def wait_bytes(ref, sem):
    pltpu.make_async_copy(ref, ref, sem).wait()


def softmax_rows(scores):
    top = jnp.max(scores, axis=-1, keepdims=True)
    weights = jnp.exp(scores - top)
    return weights / jnp.sum(weights, axis=-1, keepdims=True)


def kernel(
    q_ref, k_ref, v_ref, context_ref, residual_ref, codes_ref, scales_ref, gain_ref, weight_ref, lengths_ref,
    out_ref,
    context, residual, codes, scales, gain, weight,
    q_all, k_all, v_all, part, sums, text, squares_z, squares, rows, kv_own, kv_all, attended,
    load_sem, own_sem, send_sem, recv_sem, ready_sem,
):
    g = lax.axis_index("grp")
    me = lax.axis_index("seq")
    z, xy = me // 8, me % 8
    mine = block_of(me)

    barrier = pltpu.get_barrier_semaphore()
    for i in (4, 5, 3, 2, 6, 1, 7):
        pl.semaphore_signal(barrier, inc=1, device_id={"grp": (g + i) % 8}, device_id_type=MESH)
        pl.semaphore_signal(barrier, inc=1, device_id={"seq": partner(me, i, 0)}, device_id_type=MESH)
        pl.semaphore_signal(barrier, inc=1, device_id={"seq": partner(me, 0, i)}, device_id_type=MESH)

    loads = [
        pltpu.make_async_copy(src, dst, load_sem.at[n])
        for n, (src, dst) in enumerate(
            (
                (codes_ref, codes),
                (scales_ref, scales),
                (context_ref, context),
                (residual_ref, residual),
                (gain_ref, gain),
                (weight_ref, weight),
            )
        )
    ]
    for load in loads:
        load.start()
    arrays = ((k_ref, k_all), (q_ref, q_all), (v_ref, v_all))
    own = [pltpu.make_async_copy(src.at[mine], dst.at[:, me], own_sem.at[n]) for n, (src, dst) in enumerate(arrays)]
    for copy in own:
        copy.start()
    kv_own[...] = jnp.zeros_like(kv_own)
    squares_z[z] = jnp.zeros((2, 128), F32)

    for load in loads[:3]:
        load.wait()
    level = jnp.concatenate([jnp.broadcast_to(scales[n : n + 1, :], (128, 64)).T for n in range(4)], axis=1)
    dense = (codes[...].astype(F32) * level).astype(BF16)
    dense = jnp.concatenate([dense, dense], axis=0)
    product = dot_t(context[...], dense).reshape(8, 2, 16, 128)
    half = lax.broadcasted_iota(jnp.int32, (16, 128), 1) // 64
    first = half == me % 2
    part[...] = jnp.where(first[None], product[:, 0], product[:, 1])
    sums[g] = part[g]

    pl.semaphore_wait(barrier, 21)

    for i in (4, 5, 3, 2, 6, 1, 7):
        to = (g + i) % 8
        pltpu.make_async_remote_copy(
            part.at[to], sums.at[g], send_sem.at[0], recv_sem.at[0], device_id={"grp": to}, device_id_type=MESH
        ).start()
    for i in (4, 3, 5, 2, 6, 1, 7):
        pl.semaphore_signal(ready_sem, inc=1, device_id={"seq": partner(me, i, 0)}, device_id_type=MESH)

    def send_tokens(n, to):
        src, dst = arrays[n]
        pltpu.make_async_remote_copy(
            src.at[block_of(to)],
            dst.at[:, me],
            send_sem.at[1 + n],
            recv_sem.at[1 + n],
            device_id={"seq": to},
            device_id_type=MESH,
        ).start()

    def send_near(n):
        for i in (4, 3, 5, 2, 6, 1, 7):
            send_tokens(n, partner(me, i, 0))
            send_tokens(n, partner(me, 0, i))

    def send_part(n, low, high):
        def step(i, carry):
            send_tokens(n, partner(me, 1 + (i * 3) % 7, 1 + i // 7))
            return carry

        lax.fori_loop(low, high, step, 0)

    for n in range(3):
        send_near(n)

    loads[3].wait()
    loads[4].wait()
    start = residual[...].astype(F32)
    start = jnp.concatenate([start, start], axis=1)
    start = jnp.where(first, start[:16], start[16:])
    wide_gain = jnp.concatenate([gain[...], gain[...]], axis=1)
    pl.semaphore_wait(ready_sem, 7)
    send_part(0, 0, 28)
    wait_bytes(sums.at[0:7], recv_sem.at[0])
    hidden = start + jnp.sum(sums[...], axis=0)
    text[xy, z] = (hidden * wide_gain).astype(BF16)
    pick = lax.broadcasted_iota(jnp.int32, (2, 128), 0) == (lax.broadcasted_iota(jnp.int32, (2, 128), 1) // 64 + me) % 2
    squares_z[z, :, 0:16] = lax.dot_general(
        pick.astype(F32),
        hidden * hidden,
        (((1,), (1,)), ((), ())),
        preferred_element_type=F32,
        precision=lax.Precision.HIGHEST,
    )

    def send_line(buf, at, n, to):
        pltpu.make_async_remote_copy(
            buf.at[at], buf.at[at], send_sem.at[n], recv_sem.at[n], device_id={"seq": to}, device_id_type=MESH
        ).start()

    for i in (4, 3, 5, 2, 6, 1, 7):
        send_line(text, (xy, z), 10 + z, partner(me, i, 0))

    def forward(plane):
        for i in (5, 4, 7, 6, 3, 2, 1):
            send_line(text, (xy, plane), 6, partner(me, 0, i))

    for i in (4, 3, 5, 2, 6, 1, 7):
        send_line(squares_z, z, 5, partner(me, i, 0))

    forward(z)
    send_part(0, 28, 49)
    send_part(1, 0, 35)

    def forward_one(i, carry):
        @pl.when(i != z)
        def _():
            wait_bytes(text.at[0, 0], recv_sem.at[10 + i])
            forward(i)

        return carry

    lax.fori_loop(0, 8, forward_one, 0)
    wait_bytes(squares_z.at[0:7], recv_sem.at[5])
    squares[xy] = jnp.sum(squares_z[...], axis=0)
    for i in (5, 4, 7, 6, 3, 2, 1):
        send_line(squares, xy, 7, partner(me, 0, i))
    send_part(1, 35, 49)
    send_part(2, 0, 49)

    wait_bytes(squares.at[0:7], recv_sem.at[7])
    norm = lax.rsqrt(jnp.sum(squares[...], axis=0) / D_TEXT + 1e-06)
    diagonal = lax.broadcasted_iota(jnp.int32, (16, 128), 0) == lax.broadcasted_iota(jnp.int32, (16, 128), 1)
    norm = jnp.concatenate(
        [jnp.sum(jnp.where(diagonal, norm[n : n + 1], 0.0), axis=1, keepdims=True) for n in range(2)], axis=0
    )
    wait_bytes(text.at[0:7], recv_sem.at[6])
    left = (half == 0)[None]
    for x in range(4):
        even, odd = text[2 * x], text[2 * x + 1]
        upper = jnp.where(left, even, odd)
        lower = jnp.where(left, odd, even).astype(F32).reshape(128, 128)
        lower = pltpu.roll(lower, 64, 1).reshape(8, 16, 128).astype(BF16)
        for n in range(8):
            at = 128 * (4 * n + x)
            rows[0:16, at : at + 128] = upper[n]
            rows[16:32, at : at + 128] = lower[n]
    loads[5].wait()
    kv_own[:, 0:96] = (dot_t(rows[...], weight[...]) * norm).astype(BF16)

    prompt, triple = g // 2, (me % 32) // 4
    slot = (me // 32) * 4 + me % 4

    def send_kv(i, carry):
        to_z = (triple // 2 + 2 + 4 * (i % 2)) % 8
        to_x = (triple % 2) * 2 + prompt // 2
        pltpu.make_async_remote_copy(
            kv_own,
            kv_all.at[slot, g % 2],
            send_sem.at[8],
            recv_sem.at[8],
            device_id={"grp": i // 2, "seq": to_z * 8 + to_x * 2 + prompt % 2},
            device_id_type=MESH,
        ).start()
        return carry

    lax.fori_loop(0, 16, send_kv, 0)

    for copy in own:
        copy.wait()
    for n in range(3):
        wait_bytes(q_ref.at[0:63], recv_sem.at[1 + n])
    self_out = []
    for n in range(3):
        scores = dot_t(q_all[n].reshape(256, 128), k_all[n].reshape(256, 128)) * FACTOR
        probs = softmax_rows(scores).astype(BF16)
        self_out.append(jnp.dot(probs, v_all[n].reshape(256, 128), preferred_element_type=F32).astype(BF16))

    length = lengths_ref[(mine // 8) % 4]
    live = lax.broadcasted_iota(jnp.int32, (256, 64), 1) < length
    source = lax.broadcasted_iota(jnp.int32, (128, 384), 0)
    target = lax.broadcasted_iota(jnp.int32, (128, 384), 1)
    places = [((source + 96 * n == target) & (source < 96)).astype(BF16) for n in range(4)]
    wait_bytes(kv_all, recv_sem.at[8])
    text_keys = jnp.zeros((64, 384), F32)
    text_values = jnp.zeros((64, 384), F32)
    for n in range(4):
        text_keys += jnp.dot(kv_all[n].reshape(64, 128), places[n], preferred_element_type=F32)
        text_values += jnp.dot(kv_all[4 + n].reshape(64, 128), places[n], preferred_element_type=F32)
    text_keys, text_values = text_keys.astype(BF16), text_values.astype(BF16)
    for n in range(3):
        columns = slice(128 * n, 128 * n + 128)
        scores = dot_t(q_all[n].reshape(256, 128), text_keys[:, columns]) * FACTOR
        probs = softmax_rows(jnp.where(live, scores, -1e30)).astype(BF16)
        cross = jnp.dot(probs, text_values[:, columns], preferred_element_type=F32)
        attended[n] = (self_out[n].astype(F32) + cross).astype(BF16).reshape(64, 4, 128)

    def send_out(i, carry):
        to_z = i // 8
        to = to_z * 8 + ((xy // 2 + (i % 8) // 2) % 4) * 2 + (xy + i) % 2
        pltpu.make_async_remote_copy(
            attended.at[:, to],
            out_ref.at[mine],
            send_sem.at[9],
            recv_sem.at[9],
            device_id={"seq": to},
            device_id_type=MESH,
        ).start()
        return carry

    lax.fori_loop(0, z * 8, send_out, 0)
    lax.fori_loop(z * 8 + 1, 64, send_out, 0)
    last = pltpu.make_async_copy(attended.at[:, me], out_ref.at[mine], own_sem.at[3])
    last.start()

    wait_bytes(part.at[0:7], send_sem.at[0])
    for n in range(3):
        wait_bytes(q_ref.at[0:63], send_sem.at[1 + n])
    wait_bytes(text.at[0, 0:7], send_sem.at[10 + z])
    wait_bytes(squares_z.at[0:7], send_sem.at[5])
    wait_bytes(text.at[0:7], send_sem.at[6])
    wait_bytes(squares.at[0:7], send_sem.at[7])
    wait_bytes(kv_all, send_sem.at[8])
    last.wait()
    wait_bytes(q_ref.at[0:63], send_sem.at[9])
    wait_bytes(q_ref.at[0:63], recv_sem.at[9])


def local(queries, keys, values, context, residual, codes, scales, gain, kv_weight, lengths):
    blocks = (64, 3, 4, 128)
    anywhere = pl.BlockSpec(memory_space=pl.ANY)
    tokens = pltpu.VMEM((3, 64, 4, 128), BF16)
    out = pl.pallas_call(
        kernel,
        out_shape=pltpu.VMEM(blocks, BF16),
        in_specs=[anywhere] * 9 + [pl.BlockSpec(memory_space=pltpu.SMEM)],
        out_specs=pl.BlockSpec(memory_space=pltpu.VMEM),
        scratch_shapes=[
            pltpu.VMEM((256, 512), BF16),
            pltpu.VMEM((32, 64), BF16),
            pltpu.VMEM((64, 512), jnp.int32),
            pltpu.VMEM((4, 64), F32),
            pltpu.VMEM((1, 64), F32),
            pltpu.VMEM((96, 4096), BF16),
            tokens,
            tokens,
            tokens,
            pltpu.VMEM((8, 16, 128), F32),
            pltpu.VMEM((8, 16, 128), F32),
            pltpu.VMEM((8, 8, 16, 128), BF16),
            pltpu.VMEM((8, 2, 128), F32),
            pltpu.VMEM((8, 2, 128), F32),
            pltpu.VMEM((32, 4096), BF16),
            pltpu.VMEM((32, 128), BF16),
            pltpu.VMEM((8, 2, 32, 128), BF16),
            tokens,
            pltpu.SemaphoreType.DMA((6,)),
            pltpu.SemaphoreType.DMA((4,)),
            pltpu.SemaphoreType.DMA((18,)),
            pltpu.SemaphoreType.DMA((18,)),
            pltpu.SemaphoreType.REGULAR,
        ],
        compiler_params=pltpu.CompilerParams(
            collective_id=0, has_side_effects=True, vmem_limit_bytes=60 * 1024 * 1024
        ),
        name="block",
    )(
        queries.reshape(blocks),
        keys.reshape(blocks),
        values.reshape(blocks),
        context,
        residual,
        codes.T,
        scales,
        gain.reshape(1, 64),
        kv_weight.T,
        lengths,
    )
    return out.reshape(queries.shape)


def solution(mesh):
    placed = (
        P("grp", None, "seq", None),
        P("grp", None, "seq", None),
        P("grp", None, "seq", None),
        P(None, "grp"),
        P("grp", "seq"),
        P("grp", "seq"),
        P("grp", "seq"),
        P("seq"),
        P(None, "seq"),
        P(),
    )
    return jax.shard_map(
        local, mesh=mesh, in_specs=placed, out_specs=P("grp", None, "seq", None), check_vma=False
    )
```

```python
import math

import jax
import jax.numpy as jnp
from jax import lax
from jax.experimental import pallas as pl
from jax.experimental.pallas import tpu as pltpu
from jax.sharding import PartitionSpec as P

MESH = pl.DeviceIdType.MESH
BF16 = jnp.bfloat16
F32 = jnp.float32
FACTOR = 1.0 / math.sqrt(128)
D_TEXT = 4096


def dot_t(a, b):
    return lax.dot_general(a, b, (((1,), (1,)), ((), ())), preferred_element_type=F32)


def partner(me, dz, dxy):
    z, x, y = me // 8, (me // 2) % 4, me % 2
    return ((z + dz) % 8) * 8 + ((x + dxy // 2) % 4) * 2 + (y + dxy) % 2


def block_of(p):
    z, x, y = p // 8, (p // 2) % 4, p % 2
    t = (z + 6) % 8
    return ((t // 4) * 4 + (x % 2) * 2 + y) * 8 + (t % 4) * 2 + x // 2


def wait_bytes(ref, sem):
    pltpu.make_async_copy(ref, ref, sem).wait()


def softmax_rows(scores):
    top = jnp.max(scores, axis=-1, keepdims=True)
    weights = jnp.exp(scores - top)
    return weights / jnp.sum(weights, axis=-1, keepdims=True)


def kernel(
    q_ref, k_ref, v_ref, context_ref, residual_ref, codes_ref, scales_ref, gain_ref, weight_ref, lengths_ref,
    out_ref,
    context, residual, codes, scales, gain, weight,
    q_all, k_all, v_all, part, sums, text, squares_z, squares, rows, kv_own, kv_all, attended,
    load_sem, own_sem, send_sem, recv_sem, ready_sem,
):
    g = lax.axis_index("grp")
    me = lax.axis_index("seq")
    z, xy = me // 8, me % 8
    mine = block_of(me)

    barrier = pltpu.get_barrier_semaphore()
    for i in (4, 5, 3, 2, 6, 1, 7):
        pl.semaphore_signal(barrier, inc=1, device_id={"grp": (g + i) % 8}, device_id_type=MESH)
        pl.semaphore_signal(barrier, inc=1, device_id={"seq": partner(me, i, 0)}, device_id_type=MESH)
        pl.semaphore_signal(barrier, inc=1, device_id={"seq": partner(me, 0, i)}, device_id_type=MESH)

    loads = [
        pltpu.make_async_copy(src, dst, load_sem.at[n])
        for n, (src, dst) in enumerate(
            (
                (codes_ref, codes),
                (scales_ref, scales),
                (context_ref, context),
                (residual_ref, residual),
                (gain_ref, gain),
                (weight_ref, weight),
            )
        )
    ]
    for load in loads:
        load.start()
    arrays = ((k_ref, k_all), (q_ref, q_all), (v_ref, v_all))
    own = [pltpu.make_async_copy(src.at[mine], dst.at[:, me], own_sem.at[n]) for n, (src, dst) in enumerate(arrays)]
    for copy in own:
        copy.start()
    kv_own[...] = jnp.zeros_like(kv_own)
    squares_z[z] = jnp.zeros((2, 128), F32)

    for load in loads[:3]:
        load.wait()
    level = jnp.concatenate([jnp.broadcast_to(scales[n : n + 1, :], (128, 64)).T for n in range(4)], axis=1)
    dense = (codes[...].astype(F32) * level).astype(BF16)
    dense = jnp.concatenate([dense, dense], axis=0)
    product = dot_t(context[...], dense).reshape(8, 2, 16, 128)
    half = lax.broadcasted_iota(jnp.int32, (16, 128), 1) // 64
    first = half == me % 2
    part[...] = jnp.where(first[None], product[:, 0], product[:, 1])
    sums[g] = part[g]

    pl.semaphore_wait(barrier, 21)

    for i in (4, 5, 3, 2, 6, 1, 7):
        to = (g + i) % 8
        pltpu.make_async_remote_copy(
            part.at[to], sums.at[g], send_sem.at[0], recv_sem.at[0], device_id={"grp": to}, device_id_type=MESH
        ).start()
    for i in (4, 3, 5, 2, 6, 1, 7):
        pl.semaphore_signal(ready_sem, inc=1, device_id={"seq": partner(me, i, 0)}, device_id_type=MESH)

    def send_tokens(n, to):
        src, dst = arrays[n]
        pltpu.make_async_remote_copy(
            src.at[block_of(to)],
            dst.at[:, me],
            send_sem.at[1 + n],
            recv_sem.at[1 + n],
            device_id={"seq": to},
            device_id_type=MESH,
        ).start()

    def send_near(n):
        for i in (4, 3, 5, 2, 6, 1, 7):
            send_tokens(n, partner(me, i, 0))
            send_tokens(n, partner(me, 0, i))

    def send_part(n, low, high):
        def step(i, carry):
            send_tokens(n, partner(me, 1 + (i * 3) % 7, 1 + i // 7))
            return carry

        lax.fori_loop(low, high, step, 0)

    for n in range(3):
        send_near(n)

    loads[3].wait()
    loads[4].wait()
    start = residual[...].astype(F32)
    start = jnp.concatenate([start, start], axis=1)
    start = jnp.where(first, start[:16], start[16:])
    wide_gain = jnp.concatenate([gain[...], gain[...]], axis=1)
    pl.semaphore_wait(ready_sem, 7)
    send_part(0, 0, 28)
    wait_bytes(sums.at[0:7], recv_sem.at[0])
    hidden = start + jnp.sum(sums[...], axis=0)
    text[xy, z] = (hidden * wide_gain).astype(BF16)
    pick = lax.broadcasted_iota(jnp.int32, (2, 128), 0) == (lax.broadcasted_iota(jnp.int32, (2, 128), 1) // 64 + me) % 2
    squares_z[z, :, 0:16] = lax.dot_general(
        pick.astype(F32),
        hidden * hidden,
        (((1,), (1,)), ((), ())),
        preferred_element_type=F32,
        precision=lax.Precision.HIGHEST,
    )

    def send_line(buf, at, n, to):
        pltpu.make_async_remote_copy(
            buf.at[at], buf.at[at], send_sem.at[n], recv_sem.at[n], device_id={"seq": to}, device_id_type=MESH
        ).start()

    for i in (4, 3, 5, 2, 6, 1, 7):
        send_line(text, (xy, z), 10 + z, partner(me, i, 0))

    def forward(plane):
        for i in (5, 4, 7, 6, 3, 2, 1):
            send_line(text, (xy, plane), 6, partner(me, 0, i))

    for i in (4, 3, 5, 2, 6, 1, 7):
        send_line(squares_z, z, 5, partner(me, i, 0))

    forward(z)
    send_part(0, 28, 49)
    send_part(1, 0, 35)

    def forward_one(i, carry):
        @pl.when(i != z)
        def _():
            wait_bytes(text.at[0, 0], recv_sem.at[10 + i])
            forward(i)

        return carry

    lax.fori_loop(0, 8, forward_one, 0)
    wait_bytes(squares_z.at[0:7], recv_sem.at[5])
    squares[xy] = jnp.sum(squares_z[...], axis=0)
    for i in (5, 4, 7, 6, 3, 2, 1):
        send_line(squares, xy, 7, partner(me, 0, i))
    send_part(1, 35, 49)
    send_part(2, 0, 49)

    wait_bytes(squares.at[0:7], recv_sem.at[7])
    norm = lax.rsqrt(jnp.sum(squares[...], axis=0) / D_TEXT + 1e-06)
    diagonal = lax.broadcasted_iota(jnp.int32, (16, 128), 0) == lax.broadcasted_iota(jnp.int32, (16, 128), 1)
    norm = jnp.concatenate(
        [jnp.sum(jnp.where(diagonal, norm[n : n + 1], 0.0), axis=1, keepdims=True) for n in range(2)], axis=0
    )
    wait_bytes(text.at[0:7], recv_sem.at[6])
    left = (half == 0)[None]
    for x in range(4):
        even, odd = text[2 * x], text[2 * x + 1]
        upper = jnp.where(left, even, odd)
        lower = jnp.where(left, odd, even).astype(F32).reshape(128, 128)
        lower = pltpu.roll(lower, 64, 1).reshape(8, 16, 128).astype(BF16)
        for n in range(8):
            at = 128 * (4 * n + x)
            rows[0:16, at : at + 128] = upper[n]
            rows[16:32, at : at + 128] = lower[n]
    loads[5].wait()
    kv_own[:, 0:96] = (dot_t(rows[...], weight[...]) * norm).astype(BF16)

    prompt, triple = g // 2, (me % 32) // 4
    slot = (me // 32) * 4 + me % 4

    def send_kv(i, carry):
        to_z = (triple // 2 + 2 + 4 * (i % 2)) % 8
        to_x = (triple % 2) * 2 + prompt // 2
        pltpu.make_async_remote_copy(
            kv_own,
            kv_all.at[slot, g % 2],
            send_sem.at[8],
            recv_sem.at[8],
            device_id={"grp": i // 2, "seq": to_z * 8 + to_x * 2 + prompt % 2},
            device_id_type=MESH,
        ).start()
        return carry

    lax.fori_loop(0, 16, send_kv, 0)

    for copy in own:
        copy.wait()
    for n in range(3):
        wait_bytes(q_ref.at[0:63], recv_sem.at[1 + n])
    self_out = []
    for n in range(3):
        scores = dot_t(q_all[n].reshape(256, 128), k_all[n].reshape(256, 128)) * FACTOR
        probs = softmax_rows(scores).astype(BF16)
        self_out.append(jnp.dot(probs, v_all[n].reshape(256, 128), preferred_element_type=F32).astype(BF16))

    length = lengths_ref[(mine // 8) % 4]
    live = lax.broadcasted_iota(jnp.int32, (256, 64), 1) < length
    source = lax.broadcasted_iota(jnp.int32, (128, 384), 0)
    target = lax.broadcasted_iota(jnp.int32, (128, 384), 1)
    places = [((source + 96 * n == target) & (source < 96)).astype(BF16) for n in range(4)]
    wait_bytes(kv_all, recv_sem.at[8])
    text_keys = jnp.zeros((64, 384), F32)
    text_values = jnp.zeros((64, 384), F32)
    for n in range(4):
        text_keys += jnp.dot(kv_all[n].reshape(64, 128), places[n], preferred_element_type=F32)
        text_values += jnp.dot(kv_all[4 + n].reshape(64, 128), places[n], preferred_element_type=F32)
    text_keys, text_values = text_keys.astype(BF16), text_values.astype(BF16)
    for n in range(3):
        columns = slice(128 * n, 128 * n + 128)
        scores = dot_t(q_all[n].reshape(256, 128), text_keys[:, columns]) * FACTOR
        probs = softmax_rows(jnp.where(live, scores, -1e30)).astype(BF16)
        cross = jnp.dot(probs, text_values[:, columns], preferred_element_type=F32)
        attended[n] = (self_out[n].astype(F32) + cross).astype(BF16).reshape(64, 4, 128)

    def send_out(i, carry):
        to_z = i // 8
        to = to_z * 8 + i % 8
        pltpu.make_async_remote_copy(
            attended.at[:, to],
            out_ref.at[mine],
            send_sem.at[9],
            recv_sem.at[9],
            device_id={"seq": to},
            device_id_type=MESH,
        ).start()
        return carry

    lax.fori_loop(0, me, send_out, 0)
    lax.fori_loop(me + 1, 64, send_out, 0)
    last = pltpu.make_async_copy(attended.at[:, me], out_ref.at[mine], own_sem.at[3])
    last.start()

    wait_bytes(part.at[0:7], send_sem.at[0])
    for n in range(3):
        wait_bytes(q_ref.at[0:63], send_sem.at[1 + n])
    wait_bytes(text.at[0, 0:7], send_sem.at[10 + z])
    wait_bytes(squares_z.at[0:7], send_sem.at[5])
    wait_bytes(text.at[0:7], send_sem.at[6])
    wait_bytes(squares.at[0:7], send_sem.at[7])
    wait_bytes(kv_all, send_sem.at[8])
    last.wait()
    wait_bytes(q_ref.at[0:63], send_sem.at[9])
    wait_bytes(q_ref.at[0:63], recv_sem.at[9])


def local(queries, keys, values, context, residual, codes, scales, gain, kv_weight, lengths):
    blocks = (64, 3, 4, 128)
    anywhere = pl.BlockSpec(memory_space=pl.ANY)
    tokens = pltpu.VMEM((3, 64, 4, 128), BF16)
    out = pl.pallas_call(
        kernel,
        out_shape=pltpu.VMEM(blocks, BF16),
        in_specs=[anywhere] * 9 + [pl.BlockSpec(memory_space=pltpu.SMEM)],
        out_specs=pl.BlockSpec(memory_space=pltpu.VMEM),
        scratch_shapes=[
            pltpu.VMEM((256, 512), BF16),
            pltpu.VMEM((32, 64), BF16),
            pltpu.VMEM((64, 512), jnp.int32),
            pltpu.VMEM((4, 64), F32),
            pltpu.VMEM((1, 64), F32),
            pltpu.VMEM((96, 4096), BF16),
            tokens,
            tokens,
            tokens,
            pltpu.VMEM((8, 16, 128), F32),
            pltpu.VMEM((8, 16, 128), F32),
            pltpu.VMEM((8, 8, 16, 128), BF16),
            pltpu.VMEM((8, 2, 128), F32),
            pltpu.VMEM((8, 2, 128), F32),
            pltpu.VMEM((32, 4096), BF16),
            pltpu.VMEM((32, 128), BF16),
            pltpu.VMEM((8, 2, 32, 128), BF16),
            tokens,
            pltpu.SemaphoreType.DMA((6,)),
            pltpu.SemaphoreType.DMA((4,)),
            pltpu.SemaphoreType.DMA((18,)),
            pltpu.SemaphoreType.DMA((18,)),
            pltpu.SemaphoreType.REGULAR,
        ],
        compiler_params=pltpu.CompilerParams(
            collective_id=0, has_side_effects=True, vmem_limit_bytes=60 * 1024 * 1024
        ),
        name="block",
    )(
        queries.reshape(blocks),
        keys.reshape(blocks),
        values.reshape(blocks),
        context,
        residual,
        codes.T,
        scales,
        gain.reshape(1, 64),
        kv_weight.T,
        lengths,
    )
    return out.reshape(queries.shape)


def solution(mesh):
    placed = (
        P("grp", None, "seq", None),
        P("grp", None, "seq", None),
        P("grp", None, "seq", None),
        P(None, "grp"),
        P("grp", "seq"),
        P("grp", "seq"),
        P("grp", "seq"),
        P("seq"),
        P(None, "seq"),
        P(),
    )
    return jax.shard_map(
        local, mesh=mesh, in_specs=placed, out_specs=P("grp", None, "seq", None), check_vma=False
    )
```
